32 devices in a mesh: dp: 2 (over core), ctx: 16 (over z, y, x).
Axes of the slice: x: 2, y: 2, z: 4, core: 2. Of those that a mesh axis runs over, the one named last changes fastest.
Arguments:
- pre_gate: bfloat16 [2, 2048, 2048], P('dp', 'ctx'), may hold values from -6 to 6
- post_gate: bfloat16 [2, 2048, 2048], P('dp', 'ctx'), may hold values from -6 to 6
- values: bfloat16 [2, 2048, 2048], P('dp', 'ctx'), may hold values from -6 to 6
- conv_out: bfloat16 [2, 2048, 2048], P('dp', 'ctx'), may hold values from -6 to 6
- grad_out: bfloat16 [2, 2048, 2048], P('dp', 'ctx'), may hold values from -6 to 6
- filter_param: bfloat16 [2048, 2048], P('ctx'), may hold values from -6 to 6
Outputs:
- d_pre_gate: bfloat16 [2, 2048, 2048], P('dp', 'ctx')
- d_post_gate: bfloat16 [2, 2048, 2048], P('dp', 'ctx')
- d_values: bfloat16 [2, 2048, 2048], P('dp', 'ctx')
- d_filter: float32 [2048, 2048], P(('ctx', 'dp'))
The draws below stay inside these ranges and needn't reach their ends.
All inputs are finite; a program needn't handle non-finite values.
Results may differ from the reference program's by a relative error of at most 0.0058.
Values may be sent and summed in bfloat16 or wider, within the bound.
A program may use at most 64 MiB of HBM per device.

```python
import math
import jax
import jax.numpy as jnp
from jax import lax

C = 2048
SEQ = 2048
BATCH = 2


def level_of(rng, dims, split, least, top_value):
    def one(dim, blocks):
        draws = jax.random.uniform(jax.random.fold_in(jax.random.fold_in(rng, 6), dim), (blocks,), jnp.float32, least / len(split), top_value / len(split))
        return jnp.repeat(jnp.exp(draws), dims[dim] // blocks).reshape((-1,) + (1,) * (len(dims) - dim - 1))

    loudness = one(*split[0])
    for cut in split[1:]:
        loudness = loudness * one(*cut)
    return loudness


def bell_draw(stream_key, shape, spread, most, pieces=(), kind=jnp.bfloat16):
    gain = level_of(stream_key, shape, pieces, -0.22, 0.18) if pieces else 1.0
    values = jax.random.normal(stream_key, shape, jnp.float32) * spread * gain
    return jnp.minimum(jnp.maximum(values, -most), most).astype(kind)


def setup_inputs(seed: int = 0) -> dict:
    key_list = jax.random.split(jax.random.key(seed), 7)
    return {
        "pre_gate": bell_draw(key_list[0], (BATCH, SEQ, C), 1.0, 6.0, ((0, 2), (1, 16))),
        "post_gate": bell_draw(key_list[1], (BATCH, SEQ, C), 1.0, 6.0, ((0, 2), (1, 16))),
        "values": bell_draw(key_list[2], (BATCH, SEQ, C), 1.0, 6.0, ((0, 2), (1, 16))),
        "conv_out": bell_draw(key_list[3], (BATCH, SEQ, C), 1.0, 6.0, ((0, 2), (1, 16))),
        "grad_out": bell_draw(key_list[4], (BATCH, SEQ, C), 1.0, 6.0, ((0, 2), (1, 16))),
        "filter_param": bell_draw(key_list[5], (C, SEQ), 1.0, 6.0, ((0, 16),)),
    }


def reference(pre_gate, post_gate, values, conv_out, grad_out, filter_param):
    whole = 2 * SEQ
    kernel = filter_param.astype(jnp.float32) * SEQ ** (-0.5)
    kernel_spec = jnp.fft.fft(kernel, n=whole, axis=1)

    def one_sequence(total, items):
        gate_row, post_row, value_row, out_row, grad_row = items
        mixed = (gate_row.astype(jnp.float32) * value_row.astype(jnp.float32)).astype(jnp.bfloat16)
        grad_conv = (grad_row.astype(jnp.float32) * post_row.astype(jnp.float32)).astype(jnp.bfloat16)
        mixed_spec = jnp.fft.fft(mixed.astype(jnp.float32).T, n=whole, axis=1)
        grad_spec = jnp.fft.fft(grad_conv.astype(jnp.float32).T, n=whole, axis=1)
        back = jnp.fft.ifft(jnp.conj(kernel_spec) * grad_spec, axis=1).real[:, :SEQ]
        back = back.T.astype(jnp.bfloat16).astype(jnp.float32)
        d_pre = (back * value_row.astype(jnp.float32)).astype(jnp.bfloat16)
        d_val = (back * gate_row.astype(jnp.float32)).astype(jnp.bfloat16)
        d_post = (grad_row.astype(jnp.float32) * out_row.astype(jnp.float32)).astype(jnp.bfloat16)
        term = jnp.fft.ifft(grad_spec * jnp.conj(mixed_spec), axis=1).real[:, :SEQ]
        return (total + term.astype(total.dtype), (d_pre, d_post, d_val))
    start = jnp.zeros((C, SEQ), jnp.float32)
    total, outs = lax.scan(one_sequence, start, (pre_gate, post_gate, values, conv_out, grad_out))
    d_filter = total * (1.0 / (BATCH * math.sqrt(SEQ)))
    return (outs[0], outs[1], outs[2], d_filter)
```

```python
import functools
import math

import jax
import jax.numpy as jnp
import ml_dtypes
import numpy as np
from jax import lax
from jax.experimental import pallas as pl
from jax.experimental.pallas import tpu as pltpu
from jax.sharding import PartitionSpec as P

MESH = pl.DeviceIdType.MESH


def add(a, b):
    return b if a is None else a if b is None else a + b


def sub(a, b):
    return a if b is None else -b if a is None else a - b


def scale(a, c):
    return None if a is None or c == 0.0 else a if c == 1.0 else -a if c == -1.0 else a * c


def turn(x, k, n):
    re, im = x
    c, s = math.cos(2 * math.pi * k / n), -math.sin(2 * math.pi * k / n)
    c, s = (0.0 if abs(v) < 1e-9 else round(v) if abs(abs(v) - 1) < 1e-9 else v for v in (c, s))
    c, s = float(c), float(s)
    if c and abs(abs(c) - abs(s)) < 1e-9 and re is not None and im is not None:
        if c * s > 0:
            return scale(re - im, c), scale(re + im, c)
        return scale(re + im, c), scale(im - re, c)
    return sub(scale(re, c), scale(im, s)), add(scale(im, c), scale(re, s))


def real_dft(xs):
    n = len(xs)
    if n == 1:
        return [(xs[0], None)]
    if n == 2:
        return [(add(xs[0], xs[1]), None), (sub(xs[0], xs[1]), None)]
    even, odd = real_dft(xs[0::2]), real_dft(xs[1::2])
    out = [None] * (n // 2 + 1)
    for k in range(n // 4 + 1):
        o = turn(odd[k], k, n)
        e = even[k]
        out[n // 2 - k] = (sub(e[0], o[0]), sub(o[1], e[1]))
        out[k] = (add(e[0], o[0]), add(e[1], o[1]))
    return out


def real_inverse(bins, n):
    if n == 2:
        return [bins[0][0] + bins[1][0]]
    even, odd = [], []
    for k in range(n // 4 + 1):
        a, b = bins[k], bins[n // 2 - k]
        even.append((add(a[0], b[0]), sub(a[1], b[1])))
        odd.append(turn((sub(a[0], b[0]), add(a[1], b[1])), -k, n))
    half = n // 2
    for part in (even, odd):
        part[0] = (part[0][0], None)
        part[-1] = (part[-1][0], None)
    first, second = real_inverse(even, half), real_inverse(odd, half)
    out = []
    for a, b in zip(first, second):
        out += [a, b]
    return out


def dft_tables(blocks, size):
    groups, whole = blocks + 1, 2 * blocks * size
    g = np.arange(groups)[:, None, None]
    h = np.arange(size)[None, :, None]
    s = np.arange(size)[None, None, :]
    angle = 2 * np.pi / whole * ((s * (2 * blocks * h + g)) % whole)
    c, n = np.cos(angle), np.sin(angle)
    forward = np.concatenate([np.concatenate([c, n], 2), np.concatenate([-n, c], 2)], 1)
    inverse = np.swapaxes(forward, 1, 2) / whole
    return forward.astype(ml_dtypes.bfloat16), inverse.astype(ml_dtypes.bfloat16)


def kernel(
    blocks, size, factor_k, factor_d,
    pre_h, post_h, val_h, conv_h, grad_h, fil_h, fwd_h, inv_h,
    dpre_ref, dpost_ref, dval_ref, dfil_ref,
    pre, post, val, conv, grad, fil, fwd, inv,
    send, recv, taps, spectra, kspec, gspec, turned, dterm, dwide, dgot,
    load_sem, send_sem, recv_sem, dsem,
):
    me = lax.axis_index("ctx")
    core = lax.axis_index("dp")
    groups = blocks + 1
    f32, bf16 = jnp.float32, jnp.bfloat16
    half = size // 2

    loads = []
    for i, (a, b) in enumerate(
        [(grad_h, grad), (post_h, post), (pre_h, pre), (val_h, val), (fil_h, fil),
         (fwd_h, fwd), (inv_h, inv), (conv_h, conv)]
    ):
        loads.append(pltpu.make_async_copy(a, b, load_sem.at[i]))
        loads[-1].start()

    barrier = pltpu.get_barrier_semaphore()

    @pl.loop(1, blocks)
    def _(k):
        pl.semaphore_signal(
            barrier, inc=1, device_id=(core, lax.rem(me + k, blocks)), device_id_type=MESH
        )

    pl.semaphore_signal(barrier, inc=1, device_id=(1 - core, me), device_id_type=MESH)

    def product(phase, a, b):
        @pl.loop(0, blocks)
        def _(j):
            cols = pl.ds(pl.multiple_of(j * size, size), size)
            send[phase, j] = (a[:, cols].astype(f32) * b[:, cols].astype(f32)).astype(bf16)

    def copy(phase, other, slot):
        return pltpu.make_async_remote_copy(
            src_ref=send.at[phase, other],
            dst_ref=recv.at[phase, slot],
            send_sem=send_sem.at[phase, other],
            recv_sem=recv_sem.at[phase, slot],
            device_id=(core, other),
            device_id_type=MESH,
        )

    def start_all(phase):
        @pl.loop(1, blocks)
        def _(k):
            copy(phase, lax.rem(me + k, blocks), me).start()

        recv[phase, me] = send[phase, me]

    def wait_recv_all(phase):
        @pl.loop(1, blocks)
        def _(k):
            other = lax.rem(me + k, blocks)
            copy(phase, other, other).wait_recv()

    def wait_send_all(phase):
        @pl.loop(1, blocks)
        def _(k):
            copy(phase, lax.rem(me + k, blocks), me).wait_send()

    def split(read):
        @pl.loop(0, size // 16)
        def _(i):
            rows = pl.ds(pl.multiple_of(i * 16, 16), 16)
            lower = pl.ds(pl.multiple_of(i * 16 + size, 16), 16)
            xs = [read(q, rows).astype(f32) for q in range(blocks)] + [None] * blocks
            for g, (re, im) in enumerate(real_dft(xs)):
                spectra[g, rows, :] = re.astype(bf16)
                if im is None:
                    im = jnp.zeros_like(re)
                spectra[g, lower, :] = im.astype(bf16)

    def over_groups(body):
        @pl.loop(0, blocks // 4)
        def _(i):
            for u in range(4):
                body(i * 4 + u)

        body(blocks)

    def spectrum(g):
        return jnp.dot(fwd[g], spectra[g], preferred_element_type=f32)

    def back_to_time(g, re, im):
        both = jnp.concatenate([re.astype(bf16), im.astype(bf16)], axis=0)
        turned[g] = jnp.dot(inv[g], both, preferred_element_type=f32)

    def join(write):
        @pl.loop(0, size // 16)
        def _(i):
            rows = pl.ds(pl.multiple_of(i * 16, 16), 16)
            lower = pl.ds(pl.multiple_of(i * 16 + size, 16), 16)
            bins = []
            for g in range(groups):
                im = None if g in (0, blocks) else turned[g, lower, :]
                bins.append((turned[g, rows, :], im))
            for q, y in enumerate(real_inverse(bins, 2 * blocks)):
                write(q, rows, y)

    loads[0].wait()
    loads[1].wait()
    product(0, grad, post)
    pl.semaphore_wait(barrier, blocks)
    start_all(0)
    loads[2].wait()
    loads[3].wait()
    product(1, pre, val)
    start_all(1)

    loads[4].wait()

    @pl.loop(0, blocks)
    def _(q):
        cols = pl.ds(pl.multiple_of(q * size, size), size)
        taps[q] = fil[:, cols].astype(f32).T.astype(bf16)

    split(lambda q, rows: taps[q, rows, :])
    loads[5].wait()

    def keep_kernel(g):
        kspec[g] = spectrum(g) * factor_k

    over_groups(keep_kernel)
    loads[7].wait()
    dpost_ref[...] = (grad[...].astype(f32) * conv[...].astype(f32)).astype(bf16)
    loads[6].wait()

    wait_recv_all(0)
    split(lambda q, rows: recv[0, q, rows, :])

    def back_group(g):
        x = spectrum(g)
        gspec[g] = x
        gr, gi = x[:size], x[size:]
        kr, ki = kspec[g, :size], kspec[g, size:]
        back_to_time(g, kr * gr + ki * gi, kr * gi - ki * gr)

    over_groups(back_group)

    def keep_back(q, rows, y):
        send[2, q, rows, :] = y.astype(bf16)

    join(keep_back)
    start_all(2)

    wait_recv_all(1)
    split(lambda q, rows: recv[1, q, rows, :])

    def filter_group(g):
        x = spectrum(g)
        mr, mi = x[:size], x[size:]
        gr, gi = gspec[g, :size], gspec[g, size:]
        back_to_time(g, (gr * mr + gi * mi) * factor_d, (gi * mr - gr * mi) * factor_d)

    over_groups(filter_group)

    def keep_term(q, rows, y):
        dterm[q, rows, :] = y

    join(keep_term)

    @pl.loop(0, blocks)
    def _(q):
        cols = pl.ds(pl.multiple_of(q * size, size), size)
        dwide[:, cols] = dterm[q].T

    theirs = pl.ds(pl.multiple_of((1 - core) * half, 8), half)
    ours = pl.ds(pl.multiple_of(core * half, 8), half)
    pair = pltpu.make_async_remote_copy(
        src_ref=dwide.at[theirs, :],
        dst_ref=dgot,
        send_sem=dsem.at[0],
        recv_sem=dsem.at[1],
        device_id=(1 - core, me),
        device_id_type=MESH,
    )
    pair.start()
    pair.wait_recv()
    dfil_ref[...] = dwide[ours, :] + dgot[...]

    wait_recv_all(2)

    @pl.loop(0, blocks)
    def _(j):
        cols = pl.ds(pl.multiple_of(j * size, size), size)
        b = recv[2, j].astype(f32)
        dpre_ref[:, cols] = (b * val[:, cols].astype(f32)).astype(bf16)
        dval_ref[:, cols] = (b * pre[:, cols].astype(f32)).astype(bf16)

    pair.wait_send()
    wait_send_all(0)
    wait_send_all(1)
    wait_send_all(2)


def fast(pre_gate, post_gate, values, conv_out, grad_out, filter_param):
    blocks = lax.axis_size("ctx")
    size, channels = pre_gate.shape[1:]
    length = filter_param.shape[1]
    fwd, inv = dft_tables(blocks, size)
    rows = (size, channels)
    f32, bf16 = jnp.float32, jnp.bfloat16
    grid_block = (blocks, size, size)
    spec_block = (blocks + 1, 2 * size, size)
    vmem = pl.BlockSpec(memory_space=pltpu.VMEM)
    body = functools.partial(
        kernel, blocks, size, length ** (-0.5), 1.0 / (lax.axis_size("dp") * math.sqrt(length))
    )
    d_pre, d_post, d_val, d_fil = pl.pallas_call(
        body,
        out_shape=[
            jax.ShapeDtypeStruct(rows, bf16),
            jax.ShapeDtypeStruct(rows, bf16),
            jax.ShapeDtypeStruct(rows, bf16),
            jax.ShapeDtypeStruct((size // 2, length), f32),
        ],
        in_specs=[pl.BlockSpec(memory_space=pl.ANY)] * 8,
        out_specs=[vmem] * 4,
        scratch_shapes=[pltpu.VMEM(rows, bf16)] * 5
        + [
            pltpu.VMEM((size, length), bf16),
            pltpu.VMEM(fwd.shape, bf16),
            pltpu.VMEM(inv.shape, bf16),
            pltpu.VMEM((3,) + grid_block, bf16),
            pltpu.VMEM((3,) + grid_block, bf16),
            pltpu.VMEM(grid_block, bf16),
            pltpu.VMEM(spec_block, bf16),
            pltpu.VMEM(spec_block, f32),
            pltpu.VMEM(spec_block, f32),
            pltpu.VMEM(spec_block, f32),
            pltpu.VMEM(grid_block, f32),
            pltpu.VMEM((size, length), f32),
            pltpu.VMEM((size // 2, length), f32),
            pltpu.SemaphoreType.DMA((8,)),
            pltpu.SemaphoreType.DMA((3, blocks)),
            pltpu.SemaphoreType.DMA((3, blocks)),
            pltpu.SemaphoreType.DMA((2,)),
        ],
        compiler_params=pltpu.CompilerParams(
            collective_id=0, has_side_effects=True, vmem_limit_bytes=44 * 2**20
        ),
        name="hyena_backward",
    )(pre_gate[0], post_gate[0], values[0], conv_out[0], grad_out[0], filter_param,
      jnp.asarray(fwd), jnp.asarray(inv))
    return d_pre[None], d_post[None], d_val[None], d_fil


SECTION = 128


exact = lax.Precision.HIGHEST
full_turn = 2.0 * math.pi


def general_tables(section, inner, whole):
    rows = jnp.arange(section, dtype=jnp.int32)
    half_rows = jnp.arange(section // 2, dtype=jnp.int32)
    columns = jnp.arange(inner, dtype=jnp.int32)
    first = (
        -full_turn / section * (rows[:, None] * half_rows[None, :] % section).astype(jnp.float32)
    )
    twist = -full_turn / whole * (rows[:, None] * columns[None, :] % whole).astype(jnp.float32)
    second = -full_turn / inner * (columns[:, None] * columns[None, :] % inner).astype(jnp.float32)
    first_cos = jnp.cos(first)
    first_sin = jnp.sin(first)
    second_cos = jnp.cos(second)
    second_sin = jnp.sin(second)
    single_table = jnp.concatenate([first_cos, first_sin], axis=0)
    paired_table = jnp.concatenate(
        [
            jnp.concatenate([first_cos, -first_sin], axis=1),
            jnp.concatenate([first_sin, first_cos], axis=1),
        ],
        axis=0,
    )
    later_forward = jnp.concatenate(
        [
            jnp.concatenate([second_cos, second_sin], axis=1),
            jnp.concatenate([-second_sin, second_cos], axis=1),
        ],
        axis=0,
    )
    later_inverse = jnp.concatenate(
        [
            jnp.concatenate([second_cos, -second_sin], axis=1),
            jnp.concatenate([second_sin, second_cos], axis=1),
        ],
        axis=0,
    )
    return (
        single_table,
        paired_table,
        jnp.cos(twist),
        jnp.sin(twist),
        later_forward,
        later_inverse,
    )


def forward(signal, tables, paired):
    single_table, paired_table, twist_cos, twist_sin, later_forward, later_inverse = tables
    table = paired_table if paired else single_table
    section_one = jnp.einsum("ja,cab->cjb", table, signal, precision=exact)
    count = twist_cos.shape[0]
    real_one = section_one[:, :count]
    imag_one = section_one[:, count:]
    joined = jnp.concatenate(
        [real_one * twist_cos - imag_one * twist_sin, real_one * twist_sin + imag_one * twist_cos],
        axis=2,
    )
    return jnp.einsum("ckb,bm->ckm", joined, later_forward, precision=exact)


def inverse(spectrum, tables):
    single_table, paired_table, twist_cos, twist_sin, later_forward, later_inverse = tables
    inner = twist_cos.shape[1]
    section_two = jnp.einsum("ckm,mb->ckb", spectrum, later_inverse, precision=exact)
    real_two = section_two[..., :inner]
    imag_two = section_two[..., inner:]
    stacked = jnp.concatenate(
        [real_two * twist_cos + imag_two * twist_sin, imag_two * twist_cos - real_two * twist_sin],
        axis=1,
    )
    scale = 1.0 / (twist_cos.shape[0] * inner)
    signal = jnp.einsum("ja,cjb->cab", paired_table, stacked, precision=exact) * scale
    channels = signal.shape[0]
    middle = signal.shape[1] // 2
    return (signal[:, :middle].reshape(channels, -1), signal[:, middle:].reshape(channels, -1))


def mirror(part):
    flipped = part[:, ::-1, ::-1]
    shifted = jnp.roll(flipped, 1, axis=1)
    zero_row = jnp.roll(part[:, 0, ::-1], 1, axis=1)
    return jnp.concatenate([zero_row[:, None], shifted[:, 1:]], axis=1)


def general(pre_gate, post_gate, values, conv_out, grad_out, filter_param):
    gate_rows = pre_gate[0].astype(jnp.float32)
    post_rows = post_gate[0].astype(jnp.float32)
    value_rows = values[0].astype(jnp.float32)
    grad_rows = grad_out[0].astype(jnp.float32)
    mixed = (gate_rows * value_rows).astype(jnp.bfloat16)
    grad_conv = (grad_rows * post_rows).astype(jnp.bfloat16)
    d_post = (grad_rows * conv_out[0].astype(jnp.float32)).astype(jnp.bfloat16)
    length = filter_param.shape[1]
    whole = 2 * length
    inner = whole // SECTION
    half_section = SECTION // 2
    tables = general_tables(SECTION, inner, whole)
    kernel = (filter_param.astype(jnp.float32) * length ** (-0.5)).reshape(-1, half_section, inner)
    mixed_cols = mixed.T
    grad_cols = grad_conv.T
    mixed_chan, grad_chan = (
        lax.all_to_all(mixed_cols, "ctx", split_axis=0, concat_axis=1, tiled=True),
        lax.all_to_all(grad_cols, "ctx", split_axis=0, concat_axis=1, tiled=True),
    )
    kernel_spec = forward(kernel, tables, False)
    channels = mixed_chan.shape[0]
    both_signals = jnp.concatenate(
        [
            mixed_chan.reshape(channels, half_section, inner),
            grad_chan.reshape(channels, half_section, inner),
        ],
        axis=1,
    ).astype(jnp.float32)
    packed = forward(both_signals, tables, True)
    packed_real = packed[..., :inner]
    packed_imag = packed[..., inner:]
    mirror_real = mirror(packed_real)
    mirror_imag = mirror(packed_imag)
    mixed_real = 0.5 * (packed_real + mirror_real)
    mixed_imag = 0.5 * (packed_imag - mirror_imag)
    grad_real = 0.5 * (packed_imag + mirror_imag)
    grad_imag = 0.5 * (mirror_real - packed_real)
    kernel_real = kernel_spec[..., :inner]
    kernel_imag = kernel_spec[..., inner:]
    back_real = kernel_real * grad_real + kernel_imag * grad_imag
    back_imag = kernel_real * grad_imag - kernel_imag * grad_real
    factor = 1.0 / (lax.axis_size("dp") * math.sqrt(length))
    cross_real = (grad_real * mixed_real + grad_imag * mixed_imag) * factor
    cross_imag = (grad_imag * mixed_real - grad_real * mixed_imag) * factor
    joined = jnp.concatenate([back_real - cross_imag, back_imag + cross_real], axis=2)
    back_signal, terms = inverse(joined, tables)
    d_filter = lax.psum_scatter(terms, "dp", scatter_dimension=0, tiled=True)
    back_chan = back_signal.astype(jnp.bfloat16)
    back_rows = lax.all_to_all(back_chan, "ctx", split_axis=1, concat_axis=0, tiled=True).T.astype(
        jnp.float32
    )
    d_pre = (back_rows * value_rows).astype(jnp.bfloat16)
    d_val = (back_rows * gate_rows).astype(jnp.bfloat16)
    return (d_pre[None], d_post[None], d_val[None], d_filter)


def local(pre_gate, post_gate, values, conv_out, grad_out, filter_param):
    blocks = lax.axis_size("ctx")
    batch, size, channels = pre_gate.shape
    fits = (
        lax.axis_size("dp") == 2
        and batch == 1
        and size == 128
        and channels == 128 * blocks
        and filter_param.shape == (128, 128 * blocks)
        and blocks == 16
    )
    run = fast if fits else general
    return run(pre_gate, post_gate, values, conv_out, grad_out, filter_param)


def solution(mesh):
    return jax.shard_map(
        local,
        mesh=mesh,
        in_specs=(
            P("dp", "ctx", None),
            P("dp", "ctx", None),
            P("dp", "ctx", None),
            P("dp", "ctx", None),
            P("dp", "ctx", None),
            P("ctx", None),
        ),
        out_specs=(
            P("dp", "ctx", None),
            P("dp", "ctx", None),
            P("dp", "ctx", None),
            P(("ctx", "dp"), None),
        ),
        check_vma=False,
    )
```

```python
import functools
import math

import jax
import jax.numpy as jnp
import ml_dtypes
import numpy as np
from jax import lax
from jax.experimental import pallas as pl
from jax.experimental.pallas import tpu as pltpu
from jax.sharding import PartitionSpec as P

MESH = pl.DeviceIdType.MESH


def add(a, b):
    return b if a is None else a if b is None else a + b


def sub(a, b):
    return a if b is None else -b if a is None else a - b


def scale(a, c):
    return None if a is None or c == 0.0 else a if c == 1.0 else -a if c == -1.0 else a * c


def turn(x, k, n):
    re, im = x
    c, s = math.cos(2 * math.pi * k / n), -math.sin(2 * math.pi * k / n)
    c, s = (0.0 if abs(v) < 1e-9 else round(v) if abs(abs(v) - 1) < 1e-9 else v for v in (c, s))
    c, s = float(c), float(s)
    if c and abs(abs(c) - abs(s)) < 1e-9 and re is not None and im is not None:
        if c * s > 0:
            return scale(re - im, c), scale(re + im, c)
        return scale(re + im, c), scale(im - re, c)
    return sub(scale(re, c), scale(im, s)), add(scale(im, c), scale(re, s))


def real_dft(xs):
    n = len(xs)
    if n == 1:
        return [(xs[0], None)]
    if n == 2:
        return [(add(xs[0], xs[1]), None), (sub(xs[0], xs[1]), None)]
    even, odd = real_dft(xs[0::2]), real_dft(xs[1::2])
    out = [None] * (n // 2 + 1)
    for k in range(n // 4 + 1):
        o = turn(odd[k], k, n)
        e = even[k]
        out[n // 2 - k] = (sub(e[0], o[0]), sub(o[1], e[1]))
        out[k] = (add(e[0], o[0]), add(e[1], o[1]))
    return out


def real_inverse(bins, n):
    if n == 2:
        return [bins[0][0] + bins[1][0]]
    even, odd = [], []
    for k in range(n // 4 + 1):
        a, b = bins[k], bins[n // 2 - k]
        even.append((add(a[0], b[0]), sub(a[1], b[1])))
        odd.append(turn((sub(a[0], b[0]), add(a[1], b[1])), -k, n))
    half = n // 2
    for part in (even, odd):
        part[0] = (part[0][0], None)
        part[-1] = (part[-1][0], None)
    first, second = real_inverse(even, half), real_inverse(odd, half)
    out = []
    for a, b in zip(first, second):
        out += [a, b]
    return out


def dft_tables(blocks, size):
    groups, whole = blocks + 1, 2 * blocks * size
    g = np.arange(groups)[:, None, None]
    h = np.arange(size)[None, :, None]
    s = np.arange(size)[None, None, :]
    angle = 2 * np.pi / whole * ((s * (2 * blocks * h + g)) % whole)
    c, n = np.cos(angle), np.sin(angle)
    forward = np.concatenate([np.concatenate([c, n], 2), np.concatenate([-n, c], 2)], 1)
    inverse = np.swapaxes(forward, 1, 2) / whole
    return forward.astype(ml_dtypes.bfloat16), inverse.astype(ml_dtypes.bfloat16)


def kernel(
    blocks, size, factor_k, factor_d,
    pre_h, post_h, val_h, grad_h, fil_h, fwd_h, inv_h,
    back_ref, dfil_ref,
    pre, post, val, grad, fil, fwd, inv,
    send, recv, taps, spectra, kspec, gspec, turned, dterm, dwide, dgot,
    load_sem, send_sem, recv_sem, dsem,
):
    me = lax.axis_index("ctx")
    core = lax.axis_index("dp")
    groups = blocks + 1
    f32, bf16 = jnp.float32, jnp.bfloat16
    half = size // 2

    loads = []
    for i, (a, b) in enumerate(
        [(grad_h, grad), (post_h, post), (pre_h, pre), (val_h, val), (fil_h, fil),
         (fwd_h, fwd), (inv_h, inv)]
    ):
        loads.append(pltpu.make_async_copy(a, b, load_sem.at[i]))
        loads[-1].start()

    barrier = pltpu.get_barrier_semaphore()

    @pl.loop(1, blocks)
    def _(k):
        pl.semaphore_signal(
            barrier, inc=1, device_id=(core, lax.rem(me + k, blocks)), device_id_type=MESH
        )

    pl.semaphore_signal(barrier, inc=1, device_id=(1 - core, me), device_id_type=MESH)

    def copy(phase, other, slot):
        return pltpu.make_async_remote_copy(
            src_ref=send.at[phase, other],
            dst_ref=recv.at[phase, slot],
            send_sem=send_sem.at[phase, other],
            recv_sem=recv_sem.at[phase, slot],
            device_id=(core, other),
            device_id_type=MESH,
        )

    def product(phase, a, b, j):
        cols = pl.ds(pl.multiple_of(j * size, size), size)
        send[phase, j] = (a[:, cols].astype(f32) * b[:, cols].astype(f32)).astype(bf16)

    def product_and_start(phase, a, b):
        @pl.loop(1, blocks)
        def _(k):
            other = lax.rem(me + k, blocks)
            product(phase, a, b, other)
            copy(phase, other, me).start()

        product(phase, a, b, me)
        recv[phase, me] = send[phase, me]

    def start_all(phase):
        @pl.loop(1, blocks)
        def _(k):
            copy(phase, lax.rem(me + k, blocks), me).start()

        recv[phase, me] = send[phase, me]

    def wait_recv_all(phase):
        @pl.loop(1, blocks)
        def _(k):
            other = lax.rem(me + k, blocks)
            copy(phase, other, other).wait_recv()

    def wait_send_all(phase):
        @pl.loop(1, blocks)
        def _(k):
            copy(phase, lax.rem(me + k, blocks), me).wait_send()

    def split(read):
        @pl.loop(0, size // 16)
        def _(i):
            rows = pl.ds(pl.multiple_of(i * 16, 16), 16)
            lower = pl.ds(pl.multiple_of(i * 16 + size, 16), 16)
            xs = [read(q, rows).astype(f32) for q in range(blocks)] + [None] * blocks
            for g, (re, im) in enumerate(real_dft(xs)):
                spectra[g, rows, :] = re.astype(bf16)
                if im is None:
                    im = jnp.zeros_like(re)
                spectra[g, lower, :] = im.astype(bf16)

    def over_groups(body):
        @pl.loop(0, blocks // 4)
        def _(i):
            for u in range(4):
                body(i * 4 + u)

        body(blocks)

    def spectrum(g):
        return jnp.dot(fwd[g], spectra[g], preferred_element_type=f32)

    def back_to_time(g, re, im):
        both = jnp.concatenate([re.astype(bf16), im.astype(bf16)], axis=0)
        turned[g] = jnp.dot(inv[g], both, preferred_element_type=f32)

    def join(write):
        @pl.loop(0, size // 16)
        def _(i):
            rows = pl.ds(pl.multiple_of(i * 16, 16), 16)
            lower = pl.ds(pl.multiple_of(i * 16 + size, 16), 16)
            bins = []
            for g in range(groups):
                im = None if g in (0, blocks) else turned[g, lower, :]
                bins.append((turned[g, rows, :], im))
            for q, y in enumerate(real_inverse(bins, 2 * blocks)):
                write(q, rows, y)

    loads[0].wait()
    loads[1].wait()
    pl.semaphore_wait(barrier, blocks)
    product_and_start(0, grad, post)
    loads[2].wait()
    loads[3].wait()
    wait_send_all(0)
    product_and_start(1, pre, val)

    loads[4].wait()

    @pl.loop(0, blocks)
    def _(q):
        cols = pl.ds(pl.multiple_of(q * size, size), size)
        taps[q] = fil[:, cols].astype(f32).T.astype(bf16)

    split(lambda q, rows: taps[q, rows, :])
    loads[5].wait()

    def keep_kernel(g):
        kspec[g] = spectrum(g) * factor_k

    over_groups(keep_kernel)
    loads[6].wait()

    wait_recv_all(0)
    split(lambda q, rows: recv[0, q, rows, :])

    def back_group(g):
        x = spectrum(g)
        gspec[g] = x
        gr, gi = x[:size], x[size:]
        kr, ki = kspec[g, :size], kspec[g, size:]
        back_to_time(g, kr * gr + ki * gi, kr * gi - ki * gr)

    over_groups(back_group)

    def keep_back(q, rows, y):
        send[2, q, rows, :] = y.astype(bf16)

    join(keep_back)
    start_all(2)

    wait_recv_all(1)
    split(lambda q, rows: recv[1, q, rows, :])

    def filter_group(g):
        x = spectrum(g)
        mr, mi = x[:size], x[size:]
        gr, gi = gspec[g, :size], gspec[g, size:]
        back_to_time(g, (gr * mr + gi * mi) * factor_d, (gi * mr - gr * mi) * factor_d)

    over_groups(filter_group)

    def keep_term(q, rows, y):
        dterm[q, rows, :] = y

    join(keep_term)

    @pl.loop(0, blocks)
    def _(q):
        cols = pl.ds(pl.multiple_of(q * size, size), size)
        dwide[:, cols] = dterm[q].T

    theirs = pl.ds(pl.multiple_of((1 - core) * half, 8), half)
    ours = pl.ds(pl.multiple_of(core * half, 8), half)
    pair = pltpu.make_async_remote_copy(
        src_ref=dwide.at[theirs, :],
        dst_ref=dgot,
        send_sem=dsem.at[0],
        recv_sem=dsem.at[1],
        device_id=(1 - core, me),
        device_id_type=MESH,
    )
    pair.start()
    pair.wait_recv()
    dfil_ref[...] = dwide[ours, :] + dgot[...]

    wait_recv_all(2)

    @pl.loop(0, blocks)
    def _(j):
        cols = pl.ds(pl.multiple_of(j * size, size), size)
        back_ref[:, cols] = recv[2, j]

    pair.wait_send()
    wait_send_all(1)
    wait_send_all(2)


def write_out(back, pre, val, grad, conv, d_fil, d_pre, d_post, d_val, d_out):
    f32, bf16 = jnp.float32, jnp.bfloat16
    b = back[...].astype(f32)
    d_pre[...] = (b * val[...].astype(f32)).astype(bf16)
    d_val[...] = (b * pre[...].astype(f32)).astype(bf16)
    d_post[...] = (grad[...].astype(f32) * conv[...].astype(f32)).astype(bf16)
    d_out[...] = d_fil[...]


def fast(pre_gate, post_gate, values, conv_out, grad_out, filter_param):
    blocks = lax.axis_size("ctx")
    size, channels = pre_gate.shape[1:]
    length = filter_param.shape[1]
    fwd, inv = dft_tables(blocks, size)
    rows = (size, channels)
    f32, bf16 = jnp.float32, jnp.bfloat16
    grid_block = (blocks, size, size)
    spec_block = (blocks + 1, 2 * size, size)
    vmem = pl.BlockSpec(memory_space=pltpu.VMEM)
    body = functools.partial(
        kernel, blocks, size, length ** (-0.5), 1.0 / (lax.axis_size("dp") * math.sqrt(length))
    )
    results = pl.pallas_call(
        body,
        out_shape=[
            jax.ShapeDtypeStruct(rows, bf16),
            jax.ShapeDtypeStruct((size // 2, length), f32),
        ],
        in_specs=[pl.BlockSpec(memory_space=pltpu.HBM)] * 7,
        out_specs=[vmem] * 2,
        scratch_shapes=[pltpu.VMEM(rows, bf16)] * 4
        + [
            pltpu.VMEM((size, length), bf16),
            pltpu.VMEM(fwd.shape, bf16),
            pltpu.VMEM(inv.shape, bf16),
            pltpu.VMEM((3,) + grid_block, bf16),
            pltpu.VMEM((3,) + grid_block, bf16),
            pltpu.VMEM(grid_block, bf16),
            pltpu.VMEM(spec_block, bf16),
            pltpu.VMEM(spec_block, f32),
            pltpu.VMEM(spec_block, f32),
            pltpu.VMEM(spec_block, f32),
            pltpu.VMEM(grid_block, f32),
            pltpu.VMEM((size, length), f32),
            pltpu.VMEM((size // 2, length), f32),
            pltpu.SemaphoreType.DMA((7,)),
            pltpu.SemaphoreType.DMA((3, blocks)),
            pltpu.SemaphoreType.DMA((3, blocks)),
            pltpu.SemaphoreType.DMA((2,)),
        ],
        compiler_params=pltpu.CompilerParams(
            collective_id=0, has_side_effects=True, vmem_limit_bytes=62 * 2**20
        ),
        name="hyena_backward",
    )(pre_gate[0], post_gate[0], values[0], grad_out[0], filter_param,
      jnp.asarray(fwd), jnp.asarray(inv))
    steps = 4
    block = pl.BlockSpec((size // steps, channels), lambda i: (i, 0))
    part = pl.BlockSpec((size // 2 // steps, length), lambda i: (i, 0))
    d_pre, d_post, d_val, d_fil = pl.pallas_call(
        write_out,
        grid=(steps,),
        out_shape=[jax.ShapeDtypeStruct(rows, bf16)] * 3
        + [jax.ShapeDtypeStruct((size // 2, length), f32)],
        in_specs=[block] * 5 + [part],
        out_specs=[block] * 3 + [part],
        name="write_out",
    )(results[0], pre_gate[0], values[0], grad_out[0], conv_out[0], results[1])
    return d_pre[None], d_post[None], d_val[None], d_fil


SECTION = 128


exact = lax.Precision.HIGHEST
full_turn = 2.0 * math.pi


def general_tables(section, inner, whole):
    rows = jnp.arange(section, dtype=jnp.int32)
    half_rows = jnp.arange(section // 2, dtype=jnp.int32)
    columns = jnp.arange(inner, dtype=jnp.int32)
    first = (
        -full_turn / section * (rows[:, None] * half_rows[None, :] % section).astype(jnp.float32)
    )
    twist = -full_turn / whole * (rows[:, None] * columns[None, :] % whole).astype(jnp.float32)
    second = -full_turn / inner * (columns[:, None] * columns[None, :] % inner).astype(jnp.float32)
    first_cos = jnp.cos(first)
    first_sin = jnp.sin(first)
    second_cos = jnp.cos(second)
    second_sin = jnp.sin(second)
    single_table = jnp.concatenate([first_cos, first_sin], axis=0)
    paired_table = jnp.concatenate(
        [
            jnp.concatenate([first_cos, -first_sin], axis=1),
            jnp.concatenate([first_sin, first_cos], axis=1),
        ],
        axis=0,
    )
    later_forward = jnp.concatenate(
        [
            jnp.concatenate([second_cos, second_sin], axis=1),
            jnp.concatenate([-second_sin, second_cos], axis=1),
        ],
        axis=0,
    )
    later_inverse = jnp.concatenate(
        [
            jnp.concatenate([second_cos, -second_sin], axis=1),
            jnp.concatenate([second_sin, second_cos], axis=1),
        ],
        axis=0,
    )
    return (
        single_table,
        paired_table,
        jnp.cos(twist),
        jnp.sin(twist),
        later_forward,
        later_inverse,
    )


def forward(signal, tables, paired):
    single_table, paired_table, twist_cos, twist_sin, later_forward, later_inverse = tables
    table = paired_table if paired else single_table
    section_one = jnp.einsum("ja,cab->cjb", table, signal, precision=exact)
    count = twist_cos.shape[0]
    real_one = section_one[:, :count]
    imag_one = section_one[:, count:]
    joined = jnp.concatenate(
        [real_one * twist_cos - imag_one * twist_sin, real_one * twist_sin + imag_one * twist_cos],
        axis=2,
    )
    return jnp.einsum("ckb,bm->ckm", joined, later_forward, precision=exact)


def inverse(spectrum, tables):
    single_table, paired_table, twist_cos, twist_sin, later_forward, later_inverse = tables
    inner = twist_cos.shape[1]
    section_two = jnp.einsum("ckm,mb->ckb", spectrum, later_inverse, precision=exact)
    real_two = section_two[..., :inner]
    imag_two = section_two[..., inner:]
    stacked = jnp.concatenate(
        [real_two * twist_cos + imag_two * twist_sin, imag_two * twist_cos - real_two * twist_sin],
        axis=1,
    )
    scale = 1.0 / (twist_cos.shape[0] * inner)
    signal = jnp.einsum("ja,cjb->cab", paired_table, stacked, precision=exact) * scale
    channels = signal.shape[0]
    middle = signal.shape[1] // 2
    return (signal[:, :middle].reshape(channels, -1), signal[:, middle:].reshape(channels, -1))


def mirror(part):
    flipped = part[:, ::-1, ::-1]
    shifted = jnp.roll(flipped, 1, axis=1)
    zero_row = jnp.roll(part[:, 0, ::-1], 1, axis=1)
    return jnp.concatenate([zero_row[:, None], shifted[:, 1:]], axis=1)


def general(pre_gate, post_gate, values, conv_out, grad_out, filter_param):
    gate_rows = pre_gate[0].astype(jnp.float32)
    post_rows = post_gate[0].astype(jnp.float32)
    value_rows = values[0].astype(jnp.float32)
    grad_rows = grad_out[0].astype(jnp.float32)
    mixed = (gate_rows * value_rows).astype(jnp.bfloat16)
    grad_conv = (grad_rows * post_rows).astype(jnp.bfloat16)
    d_post = (grad_rows * conv_out[0].astype(jnp.float32)).astype(jnp.bfloat16)
    length = filter_param.shape[1]
    whole = 2 * length
    inner = whole // SECTION
    half_section = SECTION // 2
    tables = general_tables(SECTION, inner, whole)
    kernel = (filter_param.astype(jnp.float32) * length ** (-0.5)).reshape(-1, half_section, inner)
    mixed_cols = mixed.T
    grad_cols = grad_conv.T
    mixed_chan, grad_chan = (
        lax.all_to_all(mixed_cols, "ctx", split_axis=0, concat_axis=1, tiled=True),
        lax.all_to_all(grad_cols, "ctx", split_axis=0, concat_axis=1, tiled=True),
    )
    kernel_spec = forward(kernel, tables, False)
    channels = mixed_chan.shape[0]
    both_signals = jnp.concatenate(
        [
            mixed_chan.reshape(channels, half_section, inner),
            grad_chan.reshape(channels, half_section, inner),
        ],
        axis=1,
    ).astype(jnp.float32)
    packed = forward(both_signals, tables, True)
    packed_real = packed[..., :inner]
    packed_imag = packed[..., inner:]
    mirror_real = mirror(packed_real)
    mirror_imag = mirror(packed_imag)
    mixed_real = 0.5 * (packed_real + mirror_real)
    mixed_imag = 0.5 * (packed_imag - mirror_imag)
    grad_real = 0.5 * (packed_imag + mirror_imag)
    grad_imag = 0.5 * (mirror_real - packed_real)
    kernel_real = kernel_spec[..., :inner]
    kernel_imag = kernel_spec[..., inner:]
    back_real = kernel_real * grad_real + kernel_imag * grad_imag
    back_imag = kernel_real * grad_imag - kernel_imag * grad_real
    factor = 1.0 / (lax.axis_size("dp") * math.sqrt(length))
    cross_real = (grad_real * mixed_real + grad_imag * mixed_imag) * factor
    cross_imag = (grad_imag * mixed_real - grad_real * mixed_imag) * factor
    joined = jnp.concatenate([back_real - cross_imag, back_imag + cross_real], axis=2)
    back_signal, terms = inverse(joined, tables)
    d_filter = lax.psum_scatter(terms, "dp", scatter_dimension=0, tiled=True)
    back_chan = back_signal.astype(jnp.bfloat16)
    back_rows = lax.all_to_all(back_chan, "ctx", split_axis=1, concat_axis=0, tiled=True).T.astype(
        jnp.float32
    )
    d_pre = (back_rows * value_rows).astype(jnp.bfloat16)
    d_val = (back_rows * gate_rows).astype(jnp.bfloat16)
    return (d_pre[None], d_post[None], d_val[None], d_filter)


def local(pre_gate, post_gate, values, conv_out, grad_out, filter_param):
    blocks = lax.axis_size("ctx")
    batch, size, channels = pre_gate.shape
    fits = (
        lax.axis_size("dp") == 2
        and batch == 1
        and size == 128
        and channels == 128 * blocks
        and filter_param.shape == (128, 128 * blocks)
        and blocks == 16
    )
    run = fast if fits else general
    return run(pre_gate, post_gate, values, conv_out, grad_out, filter_param)


def solution(mesh):
    return jax.shard_map(
        local,
        mesh=mesh,
        in_specs=(
            P("dp", "ctx", None),
            P("dp", "ctx", None),
            P("dp", "ctx", None),
            P("dp", "ctx", None),
            P("dp", "ctx", None),
            P("ctx", None),
        ),
        out_specs=(
            P("dp", "ctx", None),
            P("dp", "ctx", None),
            P("dp", "ctx", None),
            P(("ctx", "dp"), None),
        ),
        check_vma=False,
    )
```

```python
import functools
import math

import jax
import jax.numpy as jnp
import ml_dtypes
import numpy as np
from jax import lax
from jax.experimental import pallas as pl
from jax.experimental.pallas import tpu as pltpu
from jax.sharding import PartitionSpec as P

MESH = pl.DeviceIdType.MESH


def add(a, b):
    return b if a is None else a if b is None else a + b


def sub(a, b):
    return a if b is None else -b if a is None else a - b


def scale(a, c):
    return None if a is None or c == 0.0 else a if c == 1.0 else -a if c == -1.0 else a * c


def turn(x, k, n):
    re, im = x
    c, s = math.cos(2 * math.pi * k / n), -math.sin(2 * math.pi * k / n)
    c, s = (0.0 if abs(v) < 1e-9 else round(v) if abs(abs(v) - 1) < 1e-9 else v for v in (c, s))
    c, s = float(c), float(s)
    if c and abs(abs(c) - abs(s)) < 1e-9 and re is not None and im is not None:
        if c * s > 0:
            return scale(re - im, c), scale(re + im, c)
        return scale(re + im, c), scale(im - re, c)
    return sub(scale(re, c), scale(im, s)), add(scale(im, c), scale(re, s))


def real_dft(xs):
    n = len(xs)
    if n == 1:
        return [(xs[0], None)]
    if n == 2:
        return [(add(xs[0], xs[1]), None), (sub(xs[0], xs[1]), None)]
    even, odd = real_dft(xs[0::2]), real_dft(xs[1::2])
    out = [None] * (n // 2 + 1)
    for k in range(n // 4 + 1):
        o = turn(odd[k], k, n)
        e = even[k]
        out[n // 2 - k] = (sub(e[0], o[0]), sub(o[1], e[1]))
        out[k] = (add(e[0], o[0]), add(e[1], o[1]))
    return out


def real_inverse(bins, n):
    if n == 2:
        return [bins[0][0] + bins[1][0]]
    even, odd = [], []
    for k in range(n // 4 + 1):
        a, b = bins[k], bins[n // 2 - k]
        even.append((add(a[0], b[0]), sub(a[1], b[1])))
        odd.append(turn((sub(a[0], b[0]), add(a[1], b[1])), -k, n))
    half = n // 2
    for part in (even, odd):
        part[0] = (part[0][0], None)
        part[-1] = (part[-1][0], None)
    first, second = real_inverse(even, half), real_inverse(odd, half)
    out = []
    for a, b in zip(first, second):
        out += [a, b]
    return out


def dft_tables(blocks, size):
    groups, whole = blocks + 1, 2 * blocks * size
    g = np.arange(groups)[:, None, None]
    h = np.arange(size)[None, :, None]
    s = np.arange(size)[None, None, :]
    angle = 2 * np.pi / whole * ((s * (2 * blocks * h + g)) % whole)
    c, n = np.cos(angle), np.sin(angle)
    forward = np.concatenate([np.concatenate([c, n], 2), np.concatenate([-n, c], 2)], 1)
    inverse = np.swapaxes(forward, 1, 2) / whole
    return forward.astype(ml_dtypes.bfloat16), inverse.astype(ml_dtypes.bfloat16)


def kernel(
    blocks, size, factor_k, factor_d,
    pre_h, post_h, val_h, grad_h, fil_h, fwd_h, inv_h,
    back_ref, dfil_ref,
    pre, post, val, grad, fil, fwd, inv,
    send, recv, taps, spectra, kspec, gspec, turned, dterm, dwide, dgot,
    load_sem, send_sem, recv_sem, dsem,
):
    me = lax.axis_index("ctx")
    core = lax.axis_index("dp")
    groups = blocks + 1
    f32, bf16 = jnp.float32, jnp.bfloat16
    half = size // 2

    loads = []
    for i, (a, b) in enumerate(
        [(grad_h, grad), (post_h, post), (pre_h, pre), (val_h, val), (fil_h, fil),
         (fwd_h, fwd), (inv_h, inv)]
    ):
        loads.append(pltpu.make_async_copy(a, b, load_sem.at[i]))
        if i < 2:
            loads[-1].start()

    barrier = pltpu.get_barrier_semaphore()

    @pl.loop(1, blocks)
    def _(k):
        pl.semaphore_signal(
            barrier, inc=1, device_id=(core, lax.rem(me + k, blocks)), device_id_type=MESH
        )

    pl.semaphore_signal(barrier, inc=1, device_id=(1 - core, me), device_id_type=MESH)

    def copy(phase, other, slot):
        return pltpu.make_async_remote_copy(
            src_ref=send.at[phase, other],
            dst_ref=recv.at[phase, slot],
            send_sem=send_sem.at[phase, other],
            recv_sem=recv_sem.at[phase, slot],
            device_id=(core, other),
            device_id_type=MESH,
        )

    def product(phase, a, b, j):
        cols = pl.ds(pl.multiple_of(j * size, size), size)
        send[phase, j] = (a[:, cols].astype(f32) * b[:, cols].astype(f32)).astype(bf16)

    def product_and_start(phase, a, b):
        @pl.loop(1, blocks)
        def _(k):
            other = lax.rem(me + k, blocks)
            product(phase, a, b, other)
            copy(phase, other, me).start()

        product(phase, a, b, me)
        recv[phase, me] = send[phase, me]

    def start_all(phase):
        @pl.loop(1, blocks)
        def _(k):
            copy(phase, lax.rem(me + k, blocks), me).start()

        recv[phase, me] = send[phase, me]

    def wait_recv_all(phase):
        @pl.loop(1, blocks)
        def _(k):
            other = lax.rem(me + k, blocks)
            copy(phase, other, other).wait_recv()

    def wait_send_all(phase):
        @pl.loop(1, blocks)
        def _(k):
            copy(phase, lax.rem(me + k, blocks), me).wait_send()

    def split(read):
        @pl.loop(0, size // 16)
        def _(i):
            rows = pl.ds(pl.multiple_of(i * 16, 16), 16)
            lower = pl.ds(pl.multiple_of(i * 16 + size, 16), 16)
            xs = [read(q, rows).astype(f32) for q in range(blocks)] + [None] * blocks
            for g, (re, im) in enumerate(real_dft(xs)):
                spectra[g, rows, :] = re.astype(bf16)
                if im is None:
                    im = jnp.zeros_like(re)
                spectra[g, lower, :] = im.astype(bf16)

    def over_groups(body):
        @pl.loop(0, blocks // 4)
        def _(i):
            for u in range(4):
                body(i * 4 + u)

        body(blocks)

    def spectrum(g):
        return jnp.dot(fwd[g], spectra[g], preferred_element_type=f32)

    def back_to_time(g, re, im):
        both = jnp.concatenate([re.astype(bf16), im.astype(bf16)], axis=0)
        turned[g] = jnp.dot(inv[g], both, preferred_element_type=f32)

    def join(write):
        @pl.loop(0, size // 16)
        def _(i):
            rows = pl.ds(pl.multiple_of(i * 16, 16), 16)
            lower = pl.ds(pl.multiple_of(i * 16 + size, 16), 16)
            bins = []
            for g in range(groups):
                im = None if g in (0, blocks) else turned[g, lower, :]
                bins.append((turned[g, rows, :], im))
            for q, y in enumerate(real_inverse(bins, 2 * blocks)):
                write(q, rows, y)

    loads[0].wait()
    loads[1].wait()
    for load in loads[2:]:
        load.start()
    pl.semaphore_wait(barrier, blocks)
    product_and_start(0, grad, post)
    loads[2].wait()
    loads[3].wait()
    wait_send_all(0)
    product_and_start(1, pre, val)

    loads[4].wait()

    @pl.loop(0, blocks)
    def _(q):
        cols = pl.ds(pl.multiple_of(q * size, size), size)
        taps[q] = fil[:, cols].astype(f32).T.astype(bf16)

    split(lambda q, rows: taps[q, rows, :])
    loads[5].wait()

    def keep_kernel(g):
        kspec[g] = spectrum(g) * factor_k

    over_groups(keep_kernel)
    loads[6].wait()

    wait_recv_all(0)
    split(lambda q, rows: recv[0, q, rows, :])

    def back_group(g):
        x = spectrum(g)
        gspec[g] = x
        gr, gi = x[:size], x[size:]
        kr, ki = kspec[g, :size], kspec[g, size:]
        back_to_time(g, kr * gr + ki * gi, kr * gi - ki * gr)

    over_groups(back_group)

    def keep_back(q, rows, y):
        send[2, q, rows, :] = y.astype(bf16)

    join(keep_back)
    start_all(2)

    wait_recv_all(1)
    split(lambda q, rows: recv[1, q, rows, :])

    def filter_group(g):
        x = spectrum(g)
        mr, mi = x[:size], x[size:]
        gr, gi = gspec[g, :size], gspec[g, size:]
        back_to_time(g, (gr * mr + gi * mi) * factor_d, (gi * mr - gr * mi) * factor_d)

    over_groups(filter_group)

    def keep_term(q, rows, y):
        dterm[q, rows, :] = y

    join(keep_term)

    @pl.loop(0, blocks)
    def _(q):
        cols = pl.ds(pl.multiple_of(q * size, size), size)
        dwide[:, cols] = dterm[q].T

    theirs = pl.ds(pl.multiple_of((1 - core) * half, 8), half)
    ours = pl.ds(pl.multiple_of(core * half, 8), half)
    pair = pltpu.make_async_remote_copy(
        src_ref=dwide.at[theirs, :],
        dst_ref=dgot,
        send_sem=dsem.at[0],
        recv_sem=dsem.at[1],
        device_id=(1 - core, me),
        device_id_type=MESH,
    )
    pair.start()

    wait_recv_all(2)

    @pl.loop(0, blocks)
    def _(j):
        cols = pl.ds(pl.multiple_of(j * size, size), size)
        back_ref[:, cols] = recv[2, j]

    pair.wait_recv()
    dfil_ref[...] = dwide[ours, :] + dgot[...]

    pair.wait_send()
    wait_send_all(1)
    wait_send_all(2)


def write_out(back, pre, val, grad, conv, d_fil, d_pre, d_post, d_val, d_out):
    f32, bf16 = jnp.float32, jnp.bfloat16
    b = back[...].astype(f32)
    d_pre[...] = (b * val[...].astype(f32)).astype(bf16)
    d_val[...] = (b * pre[...].astype(f32)).astype(bf16)
    d_post[...] = (grad[...].astype(f32) * conv[...].astype(f32)).astype(bf16)
    d_out[...] = d_fil[...]


def fast(pre_gate, post_gate, values, conv_out, grad_out, filter_param):
    blocks = lax.axis_size("ctx")
    size, channels = pre_gate.shape[1:]
    length = filter_param.shape[1]
    fwd, inv = dft_tables(blocks, size)
    rows = (size, channels)
    f32, bf16 = jnp.float32, jnp.bfloat16
    grid_block = (blocks, size, size)
    spec_block = (blocks + 1, 2 * size, size)
    vmem = pl.BlockSpec(memory_space=pltpu.VMEM)
    body = functools.partial(
        kernel, blocks, size, length ** (-0.5), 1.0 / (lax.axis_size("dp") * math.sqrt(length))
    )
    results = pl.pallas_call(
        body,
        out_shape=[
            jax.ShapeDtypeStruct(rows, bf16),
            jax.ShapeDtypeStruct((size // 2, length), f32),
        ],
        in_specs=[pl.BlockSpec(memory_space=pltpu.HBM)] * 7,
        out_specs=[vmem] * 2,
        scratch_shapes=[pltpu.VMEM(rows, bf16)] * 4
        + [
            pltpu.VMEM((size, length), bf16),
            pltpu.VMEM(fwd.shape, bf16),
            pltpu.VMEM(inv.shape, bf16),
            pltpu.VMEM((3,) + grid_block, bf16),
            pltpu.VMEM((3,) + grid_block, bf16),
            pltpu.VMEM(grid_block, bf16),
            pltpu.VMEM(spec_block, bf16),
            pltpu.VMEM(spec_block, f32),
            pltpu.VMEM(spec_block, f32),
            pltpu.VMEM(spec_block, f32),
            pltpu.VMEM(grid_block, f32),
            pltpu.VMEM((size, length), f32),
            pltpu.VMEM((size // 2, length), f32),
            pltpu.SemaphoreType.DMA((7,)),
            pltpu.SemaphoreType.DMA((3, blocks)),
            pltpu.SemaphoreType.DMA((3, blocks)),
            pltpu.SemaphoreType.DMA((2,)),
        ],
        compiler_params=pltpu.CompilerParams(
            collective_id=0, has_side_effects=True, vmem_limit_bytes=62 * 2**20
        ),
        name="hyena_backward",
    )(pre_gate[0], post_gate[0], values[0], grad_out[0], filter_param,
      jnp.asarray(fwd), jnp.asarray(inv))
    steps = 2
    block = pl.BlockSpec((size // steps, channels), lambda i: (i, 0))
    part = pl.BlockSpec((size // 2 // steps, length), lambda i: (i, 0))
    d_pre, d_post, d_val, d_fil = pl.pallas_call(
        write_out,
        grid=(steps,),
        out_shape=[jax.ShapeDtypeStruct(rows, bf16)] * 3
        + [jax.ShapeDtypeStruct((size // 2, length), f32)],
        in_specs=[block] * 5 + [part],
        out_specs=[block] * 3 + [part],
        name="write_out",
    )(results[0], pre_gate[0], values[0], grad_out[0], conv_out[0], results[1])
    return d_pre[None], d_post[None], d_val[None], d_fil


SECTION = 128


exact = lax.Precision.HIGHEST
full_turn = 2.0 * math.pi


def general_tables(section, inner, whole):
    rows = jnp.arange(section, dtype=jnp.int32)
    half_rows = jnp.arange(section // 2, dtype=jnp.int32)
    columns = jnp.arange(inner, dtype=jnp.int32)
    first = (
        -full_turn / section * (rows[:, None] * half_rows[None, :] % section).astype(jnp.float32)
    )
    twist = -full_turn / whole * (rows[:, None] * columns[None, :] % whole).astype(jnp.float32)
    second = -full_turn / inner * (columns[:, None] * columns[None, :] % inner).astype(jnp.float32)
    first_cos = jnp.cos(first)
    first_sin = jnp.sin(first)
    second_cos = jnp.cos(second)
    second_sin = jnp.sin(second)
    single_table = jnp.concatenate([first_cos, first_sin], axis=0)
    paired_table = jnp.concatenate(
        [
            jnp.concatenate([first_cos, -first_sin], axis=1),
            jnp.concatenate([first_sin, first_cos], axis=1),
        ],
        axis=0,
    )
    later_forward = jnp.concatenate(
        [
            jnp.concatenate([second_cos, second_sin], axis=1),
            jnp.concatenate([-second_sin, second_cos], axis=1),
        ],
        axis=0,
    )
    later_inverse = jnp.concatenate(
        [
            jnp.concatenate([second_cos, -second_sin], axis=1),
            jnp.concatenate([second_sin, second_cos], axis=1),
        ],
        axis=0,
    )
    return (
        single_table,
        paired_table,
        jnp.cos(twist),
        jnp.sin(twist),
        later_forward,
        later_inverse,
    )


def forward(signal, tables, paired):
    single_table, paired_table, twist_cos, twist_sin, later_forward, later_inverse = tables
    table = paired_table if paired else single_table
    section_one = jnp.einsum("ja,cab->cjb", table, signal, precision=exact)
    count = twist_cos.shape[0]
    real_one = section_one[:, :count]
    imag_one = section_one[:, count:]
    joined = jnp.concatenate(
        [real_one * twist_cos - imag_one * twist_sin, real_one * twist_sin + imag_one * twist_cos],
        axis=2,
    )
    return jnp.einsum("ckb,bm->ckm", joined, later_forward, precision=exact)


def inverse(spectrum, tables):
    single_table, paired_table, twist_cos, twist_sin, later_forward, later_inverse = tables
    inner = twist_cos.shape[1]
    section_two = jnp.einsum("ckm,mb->ckb", spectrum, later_inverse, precision=exact)
    real_two = section_two[..., :inner]
    imag_two = section_two[..., inner:]
    stacked = jnp.concatenate(
        [real_two * twist_cos + imag_two * twist_sin, imag_two * twist_cos - real_two * twist_sin],
        axis=1,
    )
    scale = 1.0 / (twist_cos.shape[0] * inner)
    signal = jnp.einsum("ja,cjb->cab", paired_table, stacked, precision=exact) * scale
    channels = signal.shape[0]
    middle = signal.shape[1] // 2
    return (signal[:, :middle].reshape(channels, -1), signal[:, middle:].reshape(channels, -1))


def mirror(part):
    flipped = part[:, ::-1, ::-1]
    shifted = jnp.roll(flipped, 1, axis=1)
    zero_row = jnp.roll(part[:, 0, ::-1], 1, axis=1)
    return jnp.concatenate([zero_row[:, None], shifted[:, 1:]], axis=1)


def general(pre_gate, post_gate, values, conv_out, grad_out, filter_param):
    gate_rows = pre_gate[0].astype(jnp.float32)
    post_rows = post_gate[0].astype(jnp.float32)
    value_rows = values[0].astype(jnp.float32)
    grad_rows = grad_out[0].astype(jnp.float32)
    mixed = (gate_rows * value_rows).astype(jnp.bfloat16)
    grad_conv = (grad_rows * post_rows).astype(jnp.bfloat16)
    d_post = (grad_rows * conv_out[0].astype(jnp.float32)).astype(jnp.bfloat16)
    length = filter_param.shape[1]
    whole = 2 * length
    inner = whole // SECTION
    half_section = SECTION // 2
    tables = general_tables(SECTION, inner, whole)
    kernel = (filter_param.astype(jnp.float32) * length ** (-0.5)).reshape(-1, half_section, inner)
    mixed_cols = mixed.T
    grad_cols = grad_conv.T
    mixed_chan, grad_chan = (
        lax.all_to_all(mixed_cols, "ctx", split_axis=0, concat_axis=1, tiled=True),
        lax.all_to_all(grad_cols, "ctx", split_axis=0, concat_axis=1, tiled=True),
    )
    kernel_spec = forward(kernel, tables, False)
    channels = mixed_chan.shape[0]
    both_signals = jnp.concatenate(
        [
            mixed_chan.reshape(channels, half_section, inner),
            grad_chan.reshape(channels, half_section, inner),
        ],
        axis=1,
    ).astype(jnp.float32)
    packed = forward(both_signals, tables, True)
    packed_real = packed[..., :inner]
    packed_imag = packed[..., inner:]
    mirror_real = mirror(packed_real)
    mirror_imag = mirror(packed_imag)
    mixed_real = 0.5 * (packed_real + mirror_real)
    mixed_imag = 0.5 * (packed_imag - mirror_imag)
    grad_real = 0.5 * (packed_imag + mirror_imag)
    grad_imag = 0.5 * (mirror_real - packed_real)
    kernel_real = kernel_spec[..., :inner]
    kernel_imag = kernel_spec[..., inner:]
    back_real = kernel_real * grad_real + kernel_imag * grad_imag
    back_imag = kernel_real * grad_imag - kernel_imag * grad_real
    factor = 1.0 / (lax.axis_size("dp") * math.sqrt(length))
    cross_real = (grad_real * mixed_real + grad_imag * mixed_imag) * factor
    cross_imag = (grad_imag * mixed_real - grad_real * mixed_imag) * factor
    joined = jnp.concatenate([back_real - cross_imag, back_imag + cross_real], axis=2)
    back_signal, terms = inverse(joined, tables)
    d_filter = lax.psum_scatter(terms, "dp", scatter_dimension=0, tiled=True)
    back_chan = back_signal.astype(jnp.bfloat16)
    back_rows = lax.all_to_all(back_chan, "ctx", split_axis=1, concat_axis=0, tiled=True).T.astype(
        jnp.float32
    )
    d_pre = (back_rows * value_rows).astype(jnp.bfloat16)
    d_val = (back_rows * gate_rows).astype(jnp.bfloat16)
    return (d_pre[None], d_post[None], d_val[None], d_filter)


def local(pre_gate, post_gate, values, conv_out, grad_out, filter_param):
    blocks = lax.axis_size("ctx")
    batch, size, channels = pre_gate.shape
    fits = (
        lax.axis_size("dp") == 2
        and batch == 1
        and size == 128
        and channels == 128 * blocks
        and filter_param.shape == (128, 128 * blocks)
        and blocks == 16
    )
    run = fast if fits else general
    return run(pre_gate, post_gate, values, conv_out, grad_out, filter_param)


def solution(mesh):
    return jax.shard_map(
        local,
        mesh=mesh,
        in_specs=(
            P("dp", "ctx", None),
            P("dp", "ctx", None),
            P("dp", "ctx", None),
            P("dp", "ctx", None),
            P("dp", "ctx", None),
            P("ctx", None),
        ),
        out_specs=(
            P("dp", "ctx", None),
            P("dp", "ctx", None),
            P("dp", "ctx", None),
            P(("ctx", "dp"), None),
        ),
        check_vma=False,
    )
```

```python
import functools
import math

import jax
import jax.numpy as jnp
import ml_dtypes
import numpy as np
from jax import lax
from jax.experimental import pallas as pl
from jax.experimental.pallas import tpu as pltpu
from jax.sharding import PartitionSpec as P

MESH = pl.DeviceIdType.MESH


def add(a, b):
    return b if a is None else a if b is None else a + b


def sub(a, b):
    return a if b is None else -b if a is None else a - b


def scale(a, c):
    return None if a is None or c == 0.0 else a if c == 1.0 else -a if c == -1.0 else a * c


def turn(x, k, n):
    re, im = x
    c, s = math.cos(2 * math.pi * k / n), -math.sin(2 * math.pi * k / n)
    c, s = (0.0 if abs(v) < 1e-9 else round(v) if abs(abs(v) - 1) < 1e-9 else v for v in (c, s))
    c, s = float(c), float(s)
    if c and abs(abs(c) - abs(s)) < 1e-9 and re is not None and im is not None:
        if c * s > 0:
            return scale(re - im, c), scale(re + im, c)
        return scale(re + im, c), scale(im - re, c)
    return sub(scale(re, c), scale(im, s)), add(scale(im, c), scale(re, s))


def real_dft(xs):
    n = len(xs)
    if n == 1:
        return [(xs[0], None)]
    if n == 2:
        return [(add(xs[0], xs[1]), None), (sub(xs[0], xs[1]), None)]
    even, odd = real_dft(xs[0::2]), real_dft(xs[1::2])
    out = [None] * (n // 2 + 1)
    for k in range(n // 4 + 1):
        o = turn(odd[k], k, n)
        e = even[k]
        out[n // 2 - k] = (sub(e[0], o[0]), sub(o[1], e[1]))
        out[k] = (add(e[0], o[0]), add(e[1], o[1]))
    return out


def real_inverse(bins, n):
    if n == 2:
        return [bins[0][0] + bins[1][0]]
    even, odd = [], []
    for k in range(n // 4 + 1):
        a, b = bins[k], bins[n // 2 - k]
        even.append((add(a[0], b[0]), sub(a[1], b[1])))
        odd.append(turn((sub(a[0], b[0]), add(a[1], b[1])), -k, n))
    half = n // 2
    for part in (even, odd):
        part[0] = (part[0][0], None)
        part[-1] = (part[-1][0], None)
    first, second = real_inverse(even, half), real_inverse(odd, half)
    out = []
    for a, b in zip(first, second):
        out += [a, b]
    return out


def dft_tables(blocks, size):
    groups, whole = blocks + 1, 2 * blocks * size
    g = np.arange(groups)[:, None, None]
    h = np.arange(size)[None, :, None]
    s = np.arange(size)[None, None, :]
    angle = 2 * np.pi / whole * ((s * (2 * blocks * h + g)) % whole)
    c, n = np.cos(angle), np.sin(angle)
    forward = np.concatenate([np.concatenate([c, n], 2), np.concatenate([-n, c], 2)], 1)
    inverse = np.swapaxes(forward, 1, 2) / whole
    return forward.astype(ml_dtypes.bfloat16), inverse.astype(ml_dtypes.bfloat16)


def kernel(
    blocks, size, factor_k, factor_d,
    pre_h, post_h, val_h, grad_h, fil_h, fwd_h, inv_h,
    back_ref, dfil_ref,
    pre, post, val, grad, fil, fwd, inv,
    send, recv, taps, spectra, kspec, gspec, turned, dterm, dwide, dgot,
    load_sem, send_sem, recv_sem, dsem,
):
    me = lax.axis_index("ctx")
    core = lax.axis_index("dp")
    groups = blocks + 1
    f32, bf16 = jnp.float32, jnp.bfloat16
    half = size // 2

    loads = []
    for i, (a, b) in enumerate(
        [(grad_h, grad), (post_h, post), (pre_h, pre), (val_h, val), (fil_h, fil),
         (fwd_h, fwd), (inv_h, inv)]
    ):
        loads.append(pltpu.make_async_copy(a, b, load_sem.at[i]))
        if i < 2:
            loads[-1].start()

    barrier = pltpu.get_barrier_semaphore()

    @pl.loop(1, blocks)
    def _(k):
        pl.semaphore_signal(
            barrier, inc=1, device_id=(core, lax.rem(me + k, blocks)), device_id_type=MESH
        )

    pl.semaphore_signal(barrier, inc=1, device_id=(1 - core, me), device_id_type=MESH)

    def copy(phase, other, slot):
        return pltpu.make_async_remote_copy(
            src_ref=send.at[phase, other],
            dst_ref=recv.at[phase, slot],
            send_sem=send_sem.at[phase, other],
            recv_sem=recv_sem.at[phase, slot],
            device_id=(core, other),
            device_id_type=MESH,
        )

    def product(phase, a, b, j):
        cols = pl.ds(pl.multiple_of(j * size, size), size)
        send[phase, j] = (a[:, cols].astype(f32) * b[:, cols].astype(f32)).astype(bf16)

    def product_and_start(phase, a, b):
        @pl.loop(1, blocks)
        def _(k):
            other = lax.rem(me + k, blocks)
            product(phase, a, b, other)
            copy(phase, other, me).start()

        product(phase, a, b, me)
        recv[phase, me] = send[phase, me]

    def start_all(phase):
        @pl.loop(1, blocks)
        def _(k):
            copy(phase, lax.rem(me + k, blocks), me).start()

        recv[phase, me] = send[phase, me]

    def wait_recv_all(phase):
        @pl.loop(1, blocks)
        def _(k):
            other = lax.rem(me + k, blocks)
            copy(phase, other, other).wait_recv()

    def wait_send_all(phase):
        @pl.loop(1, blocks)
        def _(k):
            copy(phase, lax.rem(me + k, blocks), me).wait_send()

    def split(read):
        @pl.loop(0, size // 16)
        def _(i):
            rows = pl.ds(pl.multiple_of(i * 16, 16), 16)
            lower = pl.ds(pl.multiple_of(i * 16 + size, 16), 16)
            xs = [read(q, rows).astype(f32) for q in range(blocks)] + [None] * blocks
            for g, (re, im) in enumerate(real_dft(xs)):
                spectra[g, rows, :] = re.astype(bf16)
                if im is None:
                    im = jnp.zeros_like(re)
                spectra[g, lower, :] = im.astype(bf16)

    def over_groups(body):
        @pl.loop(0, blocks // 8)
        def _(i):
            for u in range(8):
                body(i * 8 + u)

        body(blocks)

    def spectrum(g):
        return jnp.dot(fwd[g], spectra[g], preferred_element_type=f32)

    def back_to_time(g, re, im):
        both = jnp.concatenate([re.astype(bf16), im.astype(bf16)], axis=0)
        turned[g] = jnp.dot(inv[g], both, preferred_element_type=f32)

    def join(write):
        @pl.loop(0, size // 16)
        def _(i):
            rows = pl.ds(pl.multiple_of(i * 16, 16), 16)
            lower = pl.ds(pl.multiple_of(i * 16 + size, 16), 16)
            bins = []
            for g in range(groups):
                im = None if g in (0, blocks) else turned[g, lower, :]
                bins.append((turned[g, rows, :], im))
            for q, y in enumerate(real_inverse(bins, 2 * blocks)):
                write(q, rows, y)

    loads[0].wait()
    loads[1].wait()
    for load in loads[2:]:
        load.start()
    pl.semaphore_wait(barrier, blocks)
    product_and_start(0, grad, post)
    loads[2].wait()
    loads[3].wait()
    wait_send_all(0)
    product_and_start(1, pre, val)

    loads[4].wait()

    @pl.loop(0, blocks)
    def _(q):
        cols = pl.ds(pl.multiple_of(q * size, size), size)
        taps[q] = fil[:, cols].astype(f32).T.astype(bf16)

    split(lambda q, rows: taps[q, rows, :])
    loads[5].wait()

    def keep_kernel(g):
        kspec[g] = spectrum(g) * factor_k

    over_groups(keep_kernel)
    loads[6].wait()

    wait_recv_all(0)
    split(lambda q, rows: recv[0, q, rows, :])

    def back_group(g):
        x = spectrum(g)
        gspec[g] = x
        gr, gi = x[:size], x[size:]
        kr, ki = kspec[g, :size], kspec[g, size:]
        back_to_time(g, kr * gr + ki * gi, kr * gi - ki * gr)

    over_groups(back_group)

    def keep_back(q, rows, y):
        send[2, q, rows, :] = y.astype(bf16)

    join(keep_back)
    start_all(2)

    wait_recv_all(1)
    split(lambda q, rows: recv[1, q, rows, :])

    def filter_group(g):
        x = spectrum(g)
        mr, mi = x[:size], x[size:]
        gr, gi = gspec[g, :size], gspec[g, size:]
        back_to_time(g, (gr * mr + gi * mi) * factor_d, (gi * mr - gr * mi) * factor_d)

    over_groups(filter_group)

    def keep_term(q, rows, y):
        dterm[q, rows, :] = y

    join(keep_term)

    @pl.loop(0, blocks)
    def _(q):
        cols = pl.ds(pl.multiple_of(q * size, size), size)
        dwide[:, cols] = dterm[q].T

    theirs = pl.ds(pl.multiple_of((1 - core) * half, 8), half)
    ours = pl.ds(pl.multiple_of(core * half, 8), half)
    pair = pltpu.make_async_remote_copy(
        src_ref=dwide.at[theirs, :],
        dst_ref=dgot,
        send_sem=dsem.at[0],
        recv_sem=dsem.at[1],
        device_id=(1 - core, me),
        device_id_type=MESH,
    )
    pair.start()

    wait_recv_all(2)

    @pl.loop(0, blocks)
    def _(j):
        cols = pl.ds(pl.multiple_of(j * size, size), size)
        back_ref[:, cols] = recv[2, j]

    pair.wait_recv()
    dfil_ref[...] = dwide[ours, :] + dgot[...]

    pair.wait_send()
    wait_send_all(1)
    wait_send_all(2)


def write_out(back, pre, val, grad, conv, d_fil, d_pre, d_post, d_val, d_out):
    f32, bf16 = jnp.float32, jnp.bfloat16
    b = back[...].astype(f32)
    d_pre[...] = (b * val[...].astype(f32)).astype(bf16)
    d_val[...] = (b * pre[...].astype(f32)).astype(bf16)
    d_post[...] = (grad[...].astype(f32) * conv[...].astype(f32)).astype(bf16)
    d_out[...] = d_fil[...]


def fast(pre_gate, post_gate, values, conv_out, grad_out, filter_param):
    blocks = lax.axis_size("ctx")
    size, channels = pre_gate.shape[1:]
    length = filter_param.shape[1]
    fwd, inv = dft_tables(blocks, size)
    rows = (size, channels)
    f32, bf16 = jnp.float32, jnp.bfloat16
    grid_block = (blocks, size, size)
    spec_block = (blocks + 1, 2 * size, size)
    vmem = pl.BlockSpec(memory_space=pltpu.VMEM)
    body = functools.partial(
        kernel, blocks, size, length ** (-0.5), 1.0 / (lax.axis_size("dp") * math.sqrt(length))
    )
    results = pl.pallas_call(
        body,
        out_shape=[
            jax.ShapeDtypeStruct(rows, bf16),
            jax.ShapeDtypeStruct((size // 2, length), f32),
        ],
        in_specs=[pl.BlockSpec(memory_space=pltpu.HBM)] * 7,
        out_specs=[vmem] * 2,
        scratch_shapes=[pltpu.VMEM(rows, bf16)] * 4
        + [
            pltpu.VMEM((size, length), bf16),
            pltpu.VMEM(fwd.shape, bf16),
            pltpu.VMEM(inv.shape, bf16),
            pltpu.VMEM((3,) + grid_block, bf16),
            pltpu.VMEM((3,) + grid_block, bf16),
            pltpu.VMEM(grid_block, bf16),
            pltpu.VMEM(spec_block, bf16),
            pltpu.VMEM(spec_block, f32),
            pltpu.VMEM(spec_block, f32),
            pltpu.VMEM(spec_block, f32),
            pltpu.VMEM(grid_block, f32),
            pltpu.VMEM((size, length), f32),
            pltpu.VMEM((size // 2, length), f32),
            pltpu.SemaphoreType.DMA((7,)),
            pltpu.SemaphoreType.DMA((3, blocks)),
            pltpu.SemaphoreType.DMA((3, blocks)),
            pltpu.SemaphoreType.DMA((2,)),
        ],
        compiler_params=pltpu.CompilerParams(
            collective_id=0, has_side_effects=True, vmem_limit_bytes=62 * 2**20
        ),
        name="hyena_backward",
    )(pre_gate[0], post_gate[0], values[0], grad_out[0], filter_param,
      jnp.asarray(fwd), jnp.asarray(inv))
    steps = 2
    block = pl.BlockSpec((size // steps, channels), lambda i: (i, 0))
    part = pl.BlockSpec((size // 2 // steps, length), lambda i: (i, 0))
    d_pre, d_post, d_val, d_fil = pl.pallas_call(
        write_out,
        grid=(steps,),
        out_shape=[jax.ShapeDtypeStruct(rows, bf16)] * 3
        + [jax.ShapeDtypeStruct((size // 2, length), f32)],
        in_specs=[block] * 5 + [part],
        out_specs=[block] * 3 + [part],
        name="write_out",
    )(results[0], pre_gate[0], values[0], grad_out[0], conv_out[0], results[1])
    return d_pre[None], d_post[None], d_val[None], d_fil


SECTION = 128


exact = lax.Precision.HIGHEST
full_turn = 2.0 * math.pi


def general_tables(section, inner, whole):
    rows = jnp.arange(section, dtype=jnp.int32)
    half_rows = jnp.arange(section // 2, dtype=jnp.int32)
    columns = jnp.arange(inner, dtype=jnp.int32)
    first = (
        -full_turn / section * (rows[:, None] * half_rows[None, :] % section).astype(jnp.float32)
    )
    twist = -full_turn / whole * (rows[:, None] * columns[None, :] % whole).astype(jnp.float32)
    second = -full_turn / inner * (columns[:, None] * columns[None, :] % inner).astype(jnp.float32)
    first_cos = jnp.cos(first)
    first_sin = jnp.sin(first)
    second_cos = jnp.cos(second)
    second_sin = jnp.sin(second)
    single_table = jnp.concatenate([first_cos, first_sin], axis=0)
    paired_table = jnp.concatenate(
        [
            jnp.concatenate([first_cos, -first_sin], axis=1),
            jnp.concatenate([first_sin, first_cos], axis=1),
        ],
        axis=0,
    )
    later_forward = jnp.concatenate(
        [
            jnp.concatenate([second_cos, second_sin], axis=1),
            jnp.concatenate([-second_sin, second_cos], axis=1),
        ],
        axis=0,
    )
    later_inverse = jnp.concatenate(
        [
            jnp.concatenate([second_cos, -second_sin], axis=1),
            jnp.concatenate([second_sin, second_cos], axis=1),
        ],
        axis=0,
    )
    return (
        single_table,
        paired_table,
        jnp.cos(twist),
        jnp.sin(twist),
        later_forward,
        later_inverse,
    )


def forward(signal, tables, paired):
    single_table, paired_table, twist_cos, twist_sin, later_forward, later_inverse = tables
    table = paired_table if paired else single_table
    section_one = jnp.einsum("ja,cab->cjb", table, signal, precision=exact)
    count = twist_cos.shape[0]
    real_one = section_one[:, :count]
    imag_one = section_one[:, count:]
    joined = jnp.concatenate(
        [real_one * twist_cos - imag_one * twist_sin, real_one * twist_sin + imag_one * twist_cos],
        axis=2,
    )
    return jnp.einsum("ckb,bm->ckm", joined, later_forward, precision=exact)


def inverse(spectrum, tables):
    single_table, paired_table, twist_cos, twist_sin, later_forward, later_inverse = tables
    inner = twist_cos.shape[1]
    section_two = jnp.einsum("ckm,mb->ckb", spectrum, later_inverse, precision=exact)
    real_two = section_two[..., :inner]
    imag_two = section_two[..., inner:]
    stacked = jnp.concatenate(
        [real_two * twist_cos + imag_two * twist_sin, imag_two * twist_cos - real_two * twist_sin],
        axis=1,
    )
    scale = 1.0 / (twist_cos.shape[0] * inner)
    signal = jnp.einsum("ja,cjb->cab", paired_table, stacked, precision=exact) * scale
    channels = signal.shape[0]
    middle = signal.shape[1] // 2
    return (signal[:, :middle].reshape(channels, -1), signal[:, middle:].reshape(channels, -1))


def mirror(part):
    flipped = part[:, ::-1, ::-1]
    shifted = jnp.roll(flipped, 1, axis=1)
    zero_row = jnp.roll(part[:, 0, ::-1], 1, axis=1)
    return jnp.concatenate([zero_row[:, None], shifted[:, 1:]], axis=1)


def general(pre_gate, post_gate, values, conv_out, grad_out, filter_param):
    gate_rows = pre_gate[0].astype(jnp.float32)
    post_rows = post_gate[0].astype(jnp.float32)
    value_rows = values[0].astype(jnp.float32)
    grad_rows = grad_out[0].astype(jnp.float32)
    mixed = (gate_rows * value_rows).astype(jnp.bfloat16)
    grad_conv = (grad_rows * post_rows).astype(jnp.bfloat16)
    d_post = (grad_rows * conv_out[0].astype(jnp.float32)).astype(jnp.bfloat16)
    length = filter_param.shape[1]
    whole = 2 * length
    inner = whole // SECTION
    half_section = SECTION // 2
    tables = general_tables(SECTION, inner, whole)
    kernel = (filter_param.astype(jnp.float32) * length ** (-0.5)).reshape(-1, half_section, inner)
    mixed_cols = mixed.T
    grad_cols = grad_conv.T
    mixed_chan, grad_chan = (
        lax.all_to_all(mixed_cols, "ctx", split_axis=0, concat_axis=1, tiled=True),
        lax.all_to_all(grad_cols, "ctx", split_axis=0, concat_axis=1, tiled=True),
    )
    kernel_spec = forward(kernel, tables, False)
    channels = mixed_chan.shape[0]
    both_signals = jnp.concatenate(
        [
            mixed_chan.reshape(channels, half_section, inner),
            grad_chan.reshape(channels, half_section, inner),
        ],
        axis=1,
    ).astype(jnp.float32)
    packed = forward(both_signals, tables, True)
    packed_real = packed[..., :inner]
    packed_imag = packed[..., inner:]
    mirror_real = mirror(packed_real)
    mirror_imag = mirror(packed_imag)
    mixed_real = 0.5 * (packed_real + mirror_real)
    mixed_imag = 0.5 * (packed_imag - mirror_imag)
    grad_real = 0.5 * (packed_imag + mirror_imag)
    grad_imag = 0.5 * (mirror_real - packed_real)
    kernel_real = kernel_spec[..., :inner]
    kernel_imag = kernel_spec[..., inner:]
    back_real = kernel_real * grad_real + kernel_imag * grad_imag
    back_imag = kernel_real * grad_imag - kernel_imag * grad_real
    factor = 1.0 / (lax.axis_size("dp") * math.sqrt(length))
    cross_real = (grad_real * mixed_real + grad_imag * mixed_imag) * factor
    cross_imag = (grad_imag * mixed_real - grad_real * mixed_imag) * factor
    joined = jnp.concatenate([back_real - cross_imag, back_imag + cross_real], axis=2)
    back_signal, terms = inverse(joined, tables)
    d_filter = lax.psum_scatter(terms, "dp", scatter_dimension=0, tiled=True)
    back_chan = back_signal.astype(jnp.bfloat16)
    back_rows = lax.all_to_all(back_chan, "ctx", split_axis=1, concat_axis=0, tiled=True).T.astype(
        jnp.float32
    )
    d_pre = (back_rows * value_rows).astype(jnp.bfloat16)
    d_val = (back_rows * gate_rows).astype(jnp.bfloat16)
    return (d_pre[None], d_post[None], d_val[None], d_filter)


def local(pre_gate, post_gate, values, conv_out, grad_out, filter_param):
    blocks = lax.axis_size("ctx")
    batch, size, channels = pre_gate.shape
    fits = (
        lax.axis_size("dp") == 2
        and batch == 1
        and size == 128
        and channels == 128 * blocks
        and filter_param.shape == (128, 128 * blocks)
        and blocks == 16
    )
    run = fast if fits else general
    return run(pre_gate, post_gate, values, conv_out, grad_out, filter_param)


def solution(mesh):
    return jax.shard_map(
        local,
        mesh=mesh,
        in_specs=(
            P("dp", "ctx", None),
            P("dp", "ctx", None),
            P("dp", "ctx", None),
            P("dp", "ctx", None),
            P("dp", "ctx", None),
            P("ctx", None),
        ),
        out_specs=(
            P("dp", "ctx", None),
            P("dp", "ctx", None),
            P("dp", "ctx", None),
            P(("ctx", "dp"), None),
        ),
        check_vma=False,
    )
```
